256 devices in a mesh: rows: 64 (over z, y, core), rel: 4 (over x).
Axes of the slice: x: 4, y: 4, z: 8, core: 2. Of those that a mesh axis runs over, the one named last changes fastest.
Arguments:
- entities: float32 [131072, 400], P('rows'), may hold values from -0.6 to 0.6
- entity_state: float32 [131072], P('rows'), may hold values from 0.02 to 0.5
- relations: float32 [8, 400, 400], P('rel'), may hold values from -1.5 to 1.5
- relation_state: float32 [8, 400, 400], P('rel'), may hold values from 1 to 100
- head_block: int32 [131072, 1], P(('rows', 'rel')), may hold values from 0 to 63; in each aligned block of 512 rows (0 to 511, 512 to 1023, ...) at most 24 rows name the same one
- head_row: int32 [131072], P(('rows', 'rel')), may hold values from 0 to 2047
- tail_block: int32 [131072, 1], P(('rows', 'rel')), may hold values from 0 to 63; in each aligned block of 512 rows (0 to 511, 512 to 1023, ...) at most 24 rows name the same one
- tail_row: int32 [131072], P(('rows', 'rel')), may hold values from 0 to 2047
- rel_slot: int32 [131072], P(('rows', 'rel')), may hold values from 0 to 1
- neg_block: int32 [131072, 1], P(('rows', 'rel')), may hold values from 0 to 63; in each aligned block of 512 rows (0 to 511, 512 to 1023, ...) at most 24 rows name the same one
- neg_row: int32 [131072], P(('rows', 'rel')), may hold values from 0 to 2047
Outputs:
- new_entities: float32 [131072, 400], P('rows')
- new_entity_state: float32 [131072], P('rows')
- new_relations: float32 [8, 400, 400], P('rel')
- new_relation_state: float32 [8, 400, 400], P('rel')
The draws below stay inside these ranges and needn't reach their ends.
Inputs may be any that keep to these rules, and one draw needn't show every extreme that they name: `head_block`: among the edges of one device, no row block holds more than 24 heads; some row block holds exactly 24. `tail_block`: among the edges of one device, no row block holds more than 24 tails; some row block holds exactly 24. `neg_block`: among the negatives of one group, no row block holds more than 24; some row block holds exactly 24.
All inputs are finite; a program needn't handle non-finite values.
Results may differ from the reference program's by a relative error of at most 0.0003.
Values sent between devices are 32-bit elements; how exact they have to be, the bound alone decides.
A program may use at most 128 MiB of HBM per device.

```python
import math
import jax
import jax.numpy as jnp
import numpy as np
from jax import lax

D = 400
E_DEV = 512
NEG = 512
ENT_DEV = 2048
REL_DEV = 2
ENTITIES = 131072
EDGES = 131072
NEGS = 131072
NREL = 8
CAP_E = 24
CAP_N = 24
N_ROWS = 64
N_REL = 4


def with_ends(values, key, least, top_value):
    spot = [jax.random.randint(jax.random.fold_in(key, axis), (), 0, length) for axis, length in enumerate(values.shape)]
    widest = values.shape.index(max(values.shape))
    beside = spot[:widest] + [(spot[widest] + 1) % values.shape[widest]] + spot[widest + 1:]
    return values.at[tuple(spot)].set(least).at[tuple(beside)].set(top_value)


def level_of(rng, extent, pieces, smallest, high):
    loudness, own = 1.0, jax.random.fold_in(rng, 6)
    for dim, shards_of in pieces:
        steps = jnp.exp(jax.random.uniform(jax.random.fold_in(own, dim), (shards_of,), jnp.float32, smallest / len(pieces), high / len(pieces)))
        loudness = loudness * jnp.repeat(steps, extent[dim] // shards_of).reshape([-1 if axis == dim else 1 for axis in range(len(extent))])
    return loudness


def routed_block(rng, own, number, rows, number_of, top, most, skew):
    sequence = jax.random.permutation(rng, number_of)
    crowded, ordinary = shares(number_of, rows * top, most, skew, True), shares(number_of, rows * top, most, skew, False)
    places = jnp.arange(number_of)

    def named(sizes, turn):
        used = int((sizes > 0).sum())
        fixed = max(1, used // 4)
        moved = fixed + (places - fixed + turn * (used - fixed)) % max(1, number_of - fixed)
        return jnp.zeros((number_of,), jnp.int32).at[sequence[jnp.where(places < fixed, places, moved)]].set(jnp.asarray(sizes, jnp.int32))

    sizes = jnp.where(number % 4 == 0, named(crowded, number // 4), named(ordinary, number - number // 4 - 1))
    mixed = jax.random.permutation(jax.random.fold_in(own, 3), number_of)
    source_of, taker = mixed[0:number_of // 2 * 2:2], mixed[1:number_of // 2 * 2:2]
    slack = jnp.minimum(sizes[source_of] - 1, most - sizes[taker]) // 2
    slack = jnp.where((source_of == sequence[0]) | (taker == sequence[0]) | (sizes[taker] == 0), 0, jnp.maximum(slack, 0))
    moved = jax.random.randint(jax.random.fold_in(own, 4), (number_of // 2,), 0, 1 << 20) % (slack + 1)
    sizes = sizes.at[source_of].add(-moved).at[taker].add(moved)
    items = jnp.searchsorted(jnp.cumsum(sizes), jnp.arange(rows * top), side="right").astype(jnp.int32)
    table = items.reshape(top, rows).T
    table = table[jax.random.permutation(jax.random.fold_in(own, 1), rows)]
    turn = jax.random.randint(jax.random.fold_in(own, 2), (rows, 1), 0, top)
    return jnp.take_along_axis(table, (jnp.arange(top)[None, :] + turn) % top, axis=1)


def shares(amount, total, reach, lean, full):
    loads = [(1 << 20) // math.isqrt(rank ** lean) + 1 for rank in range(1, amount + 1)]
    largest = reach if full else min(reach, max(-(-total // amount), total * loads[0] // sum(loads)))
    least = 1 if total - largest >= amount - 1 else 0
    counts, spare = [largest] + [least] * (amount - 1), total - largest - least * (amount - 1)
    while spare > 0:
        free = [i for i in range(1, amount) if counts[i] < largest] or [i for i in range(1, amount) if counts[i] < reach]
        mass, remaining = sum([loads[i] for i in free]), spare
        for i in free:
            extra = min(reach - counts[i], max(1, remaining * loads[i] // mass), spare)
            counts[i] = counts[i] + extra
            spare = spare - extra
    return np.array(counts)


def noise(key, shape, spread, bound, shards=(), kind=jnp.bfloat16):
    values = jax.random.normal(key, shape, jnp.float32) * spread
    if len(shards) > 0:
        values = level_of(key, shape, shards, -0.22, 0.18) * values
    return jnp.clip(values, min=-bound, max=bound).astype(kind)


def setup_inputs(seed: int = 0) -> dict:
    arg_keys = jax.random.split(jax.random.key(seed), 12)
    entities = noise(arg_keys[0], (ENTITIES, D), 0.1, 0.6, ((0, 64),), jnp.float32)
    entity_state = jnp.clip(jnp.exp(math.log(0.5) - 3.218876 * jax.random.uniform(arg_keys[1], (ENTITIES,), jnp.float32) ** level_of(arg_keys[1], (ENTITIES,), ((0, 64),), -0.2, 0.2)), 0.02, 0.5)
    relations = noise(arg_keys[2], (NREL, D, D), 0.25, 1.5, ((0, 4),), jnp.float32)
    relation_state = jnp.clip(jnp.exp(math.log(100.0) - 4.6051702 * jax.random.uniform(arg_keys[3], (NREL, D, D), jnp.float32) ** level_of(arg_keys[3], (NREL, D, D), ((0, 4),), -0.2, 0.2)), 1.0, 100.0)
    head_block_keys = jax.random.split(jax.random.fold_in(arg_keys[4], 1), EDGES // E_DEV)
    head_block_turns = jax.random.permutation(jax.random.fold_in(arg_keys[4], 3), EDGES // E_DEV)
    head_block = jax.vmap(lambda own, number: routed_block(jax.random.fold_in(arg_keys[4], 2), own, number, E_DEV, N_ROWS, 1, CAP_E, 2))(head_block_keys, head_block_turns).reshape((EDGES, 1))
    head_row = with_ends(jax.random.randint(arg_keys[5], (EDGES,), 0, ENT_DEV), jax.random.fold_in(arg_keys[5], 1), 0, ENT_DEV - 1).astype(jnp.int32)
    tail_block_keys = jax.random.split(jax.random.fold_in(arg_keys[6], 1), EDGES // E_DEV)
    tail_block_turns = jax.random.permutation(jax.random.fold_in(arg_keys[6], 3), EDGES // E_DEV)
    tail_block = jax.vmap(lambda own, number: routed_block(jax.random.fold_in(arg_keys[6], 2), own, number, E_DEV, N_ROWS, 1, CAP_E, 2))(tail_block_keys, tail_block_turns).reshape((EDGES, 1))
    tail_row = with_ends(jax.random.randint(arg_keys[7], (EDGES,), 0, ENT_DEV), jax.random.fold_in(arg_keys[7], 1), 0, ENT_DEV - 1).astype(jnp.int32)
    rel_slot = with_ends(jax.random.randint(arg_keys[8], (EDGES,), 0, REL_DEV), jax.random.fold_in(arg_keys[8], 1), 0, REL_DEV - 1).astype(jnp.int32)
    neg_block_keys = jax.random.split(jax.random.fold_in(arg_keys[9], 1), NEGS // NEG)
    neg_block_turns = jax.random.permutation(jax.random.fold_in(arg_keys[9], 3), NEGS // NEG)
    neg_block = jax.vmap(lambda own, number: routed_block(jax.random.fold_in(arg_keys[9], 2), own, number, NEG, N_ROWS, 1, CAP_N, 1))(neg_block_keys, neg_block_turns).reshape((NEGS, 1))
    neg_row = with_ends(jax.random.randint(arg_keys[10], (NEGS,), 0, ENT_DEV), jax.random.fold_in(arg_keys[10], 1), 0, ENT_DEV - 1).astype(jnp.int32)
    return {"entities": entities, "entity_state": entity_state, "relations": relations, "relation_state": relation_state, "head_block": head_block, "head_row": head_row, "tail_block": tail_block, "tail_row": tail_row, "rel_slot": rel_slot, "neg_block": neg_block, "neg_row": neg_row}


highest = lax.Precision.HIGHEST
entity_rate = 0.1
relation_rate = 0.1

def edge_grads(head_vecs, tail_vecs, neg_vecs, rel_pair, slot_ids):
    choices_count = rel_pair.shape[0]
    member = (slot_ids[:, None] == jnp.arange(choices_count, dtype=jnp.int32)[None, :]).astype(jnp.float32)
    products = jnp.einsum('ed,kdf->kef', head_vecs, rel_pair, precision=highest)
    projected = jnp.einsum('ek,kef->ef', member, products, precision=highest)
    pos_score = lax.optimization_barrier(jnp.sum(projected * tail_vecs, axis=-1))
    neg_score = jnp.dot(projected, neg_vecs.T, precision=highest)
    pos_weight = -jax.nn.sigmoid(-pos_score)
    neg_weight = jax.nn.sigmoid(neg_score) / neg_vecs.shape[0]
    proj_grad = pos_weight[:, None] * tail_vecs + jnp.dot(neg_weight, neg_vecs, precision=highest)
    backward = jnp.einsum('ef,kdf->ked', proj_grad, rel_pair, precision=highest)
    head_grad = jnp.einsum('ek,ked->ed', member, backward, precision=highest)
    tail_grad = pos_weight[:, None] * projected
    neg_grad = jnp.dot(neg_weight.T, projected, precision=highest)
    rel_grad = jnp.einsum('ed,ek,ef->kdf', head_vecs, member, proj_grad, precision=highest)
    return (head_grad, tail_grad, neg_grad, rel_grad)

def reference(entities, entity_state, relations, relation_state, head_block, head_row, tail_block, tail_row, rel_slot, neg_block, neg_row):
    head_ids = (head_block[:, 0] * ENT_DEV + head_row).astype(jnp.int32)
    tail_ids = (tail_block[:, 0] * ENT_DEV + tail_row).astype(jnp.int32)
    neg_ids = (neg_block[:, 0] * ENT_DEV + neg_row).astype(jnp.int32)
    group_total = N_ROWS * N_REL

    def advance(carry, index):
        ent_grad, rel_grad = carry
        edge_start = (index * E_DEV).astype(jnp.int32)
        neg_start = (index * NEG).astype(jnp.int32)
        owner_start = (index % N_REL * REL_DEV).astype(jnp.int32)
        head_part = lax.dynamic_slice_in_dim(head_ids, edge_start, E_DEV)
        tail_part = lax.dynamic_slice_in_dim(tail_ids, edge_start, E_DEV)
        slot_part = lax.dynamic_slice_in_dim(rel_slot, edge_start, E_DEV)
        neg_part = lax.dynamic_slice_in_dim(neg_ids, neg_start, NEG)
        rel_pair = lax.dynamic_slice_in_dim(relations, owner_start, REL_DEV, 0)
        head_grad, tail_grad, neg_grad, pair_grad = edge_grads(entities[head_part], entities[tail_part], entities[neg_part], rel_pair, slot_part)
        ent_grad = ent_grad.at[head_part].add(head_grad).at[tail_part].add(tail_grad).at[neg_part].add(neg_grad)
        before = lax.dynamic_slice_in_dim(rel_grad, owner_start, REL_DEV, 0)
        rel_grad = lax.dynamic_update_slice_in_dim(rel_grad, before + pair_grad, owner_start, 0)
        return ((ent_grad, rel_grad), None)
    start_carry = (jnp.zeros((ENTITIES, D), jnp.float32), jnp.zeros((NREL, D, D), jnp.float32))
    (ent_grad, rel_grad), unused = lax.scan(advance, start_carry, jnp.arange(group_total, dtype=jnp.int32))
    new_entity_state = entity_state + lax.optimization_barrier(jnp.mean(ent_grad * ent_grad, axis=1))
    new_entities = entities - entity_rate * ent_grad / jnp.sqrt(new_entity_state)[:, None]
    new_relation_state = relation_state + rel_grad * rel_grad
    new_relations = relations - relation_rate * rel_grad / jnp.sqrt(new_relation_state)
    return (new_entities, new_entity_state, new_relations, new_relation_state)
```

```python
import functools

import jax
import jax.numpy as jnp
from jax import lax
from jax.experimental import pallas as pl
from jax.experimental.pallas import tpu as pltpu
from jax.sharding import PartitionSpec as P

MESH = pl.DeviceIdType.MESH
entity_rate = 0.1
relation_rate = 0.1
LANES = 128
NZ = 8
VMEM_LIMIT = 56 * 2**20
f32, bf16 = jnp.float32, jnp.bfloat16


def split(x):
    hi = x.astype(bf16)
    return hi, (x - hi.astype(f32)).astype(bf16)


def mm(a, b, dims=((1,), (0,))):
    return lax.dot_general(a, b, (dims, ((), ())), preferred_element_type=f32)


def mm3(a, b, dims=((1,), (0,))):
    ah, al = a
    bh, bl = b
    return mm(ah, bh, dims) + (mm(ah, bl, dims) + mm(al, bh, dims))


def iota(shape, axis):
    return lax.broadcasted_iota(jnp.int32, shape, axis)


def as_column(row, n):
    return jnp.sum(
        jnp.where(iota((n, n), 0) == iota((n, n), 1), jnp.broadcast_to(row, (n, n)), 0.0),
        axis=1,
        keepdims=True,
    )


def as_row(column, n):
    return jnp.sum(
        jnp.where(iota((n, n), 0) == iota((n, n), 1), jnp.broadcast_to(column, (n, n)), 0.0),
        axis=0,
        keepdims=True,
    )


def route_kernel(cap, hb, tb, nb, rows, want_ref, slot_ref):
    n = hb.shape[0]
    owners = want_ref.shape[0]
    before = (iota((n, n), 1) < iota((n, n), 0)).astype(bf16)
    lists = jnp.zeros((owners, LANES), f32)
    slots = jnp.zeros((n, LANES), f32)
    lane = iota((n, LANES), 1).astype(f32)
    for s, ref in enumerate((hb, tb, nb)):
        block = ref[...].astype(f32)
        member = lane == block
        earlier = mm(before, member.astype(bf16))
        pos = jnp.sum(jnp.where(member, earlier, 0.0), axis=1, keepdims=True)
        slots = jnp.where(lane == s, block * cap + pos, slots)
        value = as_column(rows[s : s + 1, :].astype(f32), n) + 1.0
        high = jnp.floor(value * (1.0 / 64.0))
        low = value - 64.0 * high
        at = lane == pos + float(cap * s)
        to_owner = (iota((owners, n), 0).astype(f32) == as_row(block, n)).astype(bf16)
        lists = (
            lists
            + 64.0 * mm(to_owner, jnp.where(at, high, 0.0).astype(bf16))
            + mm(to_owner, jnp.where(at, low, 0.0).astype(bf16))
        )
    slots = jnp.where(lane == 3, as_column(rows[3:4, :].astype(f32), n), slots)
    want_ref[...] = jnp.broadcast_to((lists - 1.0)[:, None, :], want_ref.shape)
    slot_ref[...] = slots


def partner(b, j, sign, nyc):
    me = lax.axis_index("rows")
    z, yc = me // nyc, me % nyc
    dz = (j + 1) // 2 if j % 2 else (NZ - j // 2) % NZ
    if sign > 0:
        return ((z + dz) % NZ) * nyc + (yc + b + j) % nyc
    return ((z + NZ - dz) % NZ) * nyc + (yc + 2 * nyc - b - j % nyc) % nyc


def meet_all(nyc):
    barrier = pltpu.get_barrier_semaphore()

    def greet(b, carry):
        for j in range(NZ):
            p = partner(b, j, 1, nyc)

            def tell():
                pl.semaphore_signal(barrier, inc=1, device_id={"rows": p}, device_id_type=MESH)

            if j == 0:
                pl.when(b > 0)(tell)
            else:
                tell()
        return carry

    lax.fori_loop(0, nyc, greet, 0)
    pl.semaphore_wait(barrier, NZ * nyc - 1)


def for_others(nyc, sign, body):
    def step(b, carry):
        for j in range(NZ):
            p = partner(b, j, sign, nyc)
            if j == 0:
                pl.when(b > 0)(functools.partial(body, p))
            else:
                body(p)
        return carry

    lax.fori_loop(0, nyc, step, 0)


def remote(src, dst, send, recv, p):
    return pltpu.make_async_remote_copy(
        src_ref=src, dst_ref=dst, send_sem=send, recv_sem=recv, device_id={"rows": p}, device_id_type=MESH
    )


def fetch_kernel(
    want, ent, fetched, asked, hi, lo, stage, isend, irecv, send, recv
):
    me = lax.axis_index("rows")
    owners = want.shape[0]
    nyc = owners // NZ
    rows, width = ent.shape
    full = width // LANES * LANES
    slots = 72
    meet_all(nyc)

    def index_copy(p, slot):
        return remote(want.at[p], asked.at[slot], isend.at[p], irecv.at[slot], p)

    for_others(nyc, 1, lambda p: index_copy(p, me).start())
    asked[me] = want[me]

    def cut(i, carry):
        at = pl.ds(pl.multiple_of(i * 256, 256), 256)
        h, l = split(ent[at, :full])
        hi[at, :full] = h
        lo[at, :full] = l
        hi[at, full:] = jnp.zeros((256, LANES), bf16)
        lo[at, full:] = jnp.zeros((256, LANES), bf16)
        h, l = split(ent[at, full:])
        hi[at, full:width] = h
        lo[at, full:width] = l
        return carry

    lax.fori_loop(0, rows // 256, cut, 0)
    for_others(nyc, 1, lambda p: index_copy(p, p).wait_recv())
    chunk = 512

    def answer(b, carry):
        to = [partner(b, j, 1, nyc) for j in range(NZ)]
        ids = jnp.concatenate([as_column(asked[p][0:1, :], LANES)[:slots] for p in to], axis=0)
        ids = ids.astype(jnp.int32)

        def gather(c, total):
            at = pl.ds(pl.multiple_of(c * chunk, chunk), chunk)
            pick = (ids - c * chunk == iota((NZ * slots, chunk), 1)).astype(bf16)
            return total + (mm(pick, hi[at, :]) + mm(pick, lo[at, :]))

        found = lax.fori_loop(
            0, rows // chunk, gather, jnp.zeros((NZ * slots, full + LANES), f32)
        )
        for j, p in enumerate(to):
            pack(stage, p, found[j * slots : (j + 1) * slots])
            copy = remote(stage.at[p], fetched.at[me], send.at[p], recv.at[me], p)
            if j == 0:
                pl.when(b > 0)(copy.start)
            else:
                copy.start()
        return carry

    lax.fori_loop(0, nyc, answer, 0)
    fetched[me] = stage[me]

    def finish(p):
        index_copy(p, p).wait_send()
        copy = remote(stage.at[p], fetched.at[p], send.at[p], recv.at[p], p)
        copy.wait_send()
        copy.wait_recv()

    for_others(nyc, 1, finish)


def pack(ref, p, block):
    slots = block.shape[0]
    planes = block.shape[1] // LANES - 1
    for c in range(planes):
        ref[p, c * slots : (c + 1) * slots, :] = block[:, c * LANES : (c + 1) * LANES]
    tail = block[:, planes * LANES :]
    packed = tail[0:8]
    for g in range(1, 8):
        packed = packed + pltpu.roll(tail[8 * g : 8 * g + 8], 16 * g, 1)
    ref[p, planes * slots : planes * slots + 8, :] = packed
    ref[p, planes * slots + 8 : planes * slots + 16, :] = tail[64:72]


def unpack_tail(ref, p, base):
    packed = ref[p, base : base + 8, :]
    low = iota((8, LANES), 1) < 16
    parts = [jnp.where(low, packed, 0.0)]
    for g in range(1, 8):
        parts.append(jnp.where(low, pltpu.roll(packed, LANES - 16 * g, 1), 0.0))
    parts.append(ref[p, base + 8 : base + 16, :])
    return jnp.concatenate(parts, axis=0)


def edge_kernel(
    fetched, rel, slots, out, rel_grad, xh, xl, vecs, grads, whole, rh, rl
):
    owners = fetched.shape[0]
    edges = slots.shape[0]
    width = rel.shape[1]
    full = width // LANES * LANES
    wide = full + LANES
    cap = 3 * edges // owners
    per = 3 * cap
    base = full // LANES * per
    total = owners * cap
    step = min(256, edges)
    low8 = iota((8, LANES), 1) < 16

    rh[...] = jnp.zeros(rh.shape, bf16)
    rl[...] = jnp.zeros(rl.shape, bf16)
    for k in range(rel.shape[0]):
        h, l = split(rel[k])
        rh[k, :width, :width] = h
        rl[k, :width, :width] = l

    for s in range(3):

        def collect(i, carry, s=s):
            at = pl.ds(pl.multiple_of(i * 8 * cap, 8 * cap), 8 * cap)
            from_ = pl.ds(i * 8, 8)
            for c in range(full // LANES):
                v = fetched[from_, c * per + s * cap : c * per + (s + 1) * cap, :]
                h, l = split(v.reshape(8 * cap, LANES))
                xh[at, c * LANES : (c + 1) * LANES] = h
                xl[at, c * LANES : (c + 1) * LANES] = l
            packed = fetched[from_, base : base + 8, :].reshape(64, LANES)
            low = iota((64, LANES), 1) < 16
            parts = []
            for g in range(3 * s, 3 * s + 3):
                if g == 8:
                    part = fetched[from_, base + 8 : base + 16, :].reshape(64, LANES)
                elif g == 0:
                    part = jnp.where(low, packed, 0.0)
                else:
                    part = jnp.where(low, pltpu.roll(packed, LANES - 16 * g, 1), 0.0)
                parts.append(part.reshape(8, 1, 8, LANES))
            h, l = split(jnp.concatenate(parts, axis=1).reshape(8 * cap, LANES))
            xh[at, full:] = h
            xl[at, full:] = l
            return carry

        lax.fori_loop(0, owners // 8, collect, 0)

        def choose(i, carry, s=s):
            at = pl.ds(pl.multiple_of(i * step, step), step)
            place = slots[at, :][:, s : s + 1].astype(jnp.int32)
            pick = (place == iota((step, total), 1)).astype(bf16)
            vecs[s, at, :] = mm(pick, xh[...]) + mm(pick, xl[...])
            return carry

        lax.fori_loop(0, edges // step, choose, 0)

    grads[2] = jnp.zeros((edges, wide), f32)
    whole[0:wide] = jnp.zeros((wide, wide), f32)
    whole[wide : 2 * wide] = jnp.zeros((wide, wide), f32)
    last = ((1,), (1,))

    def grad(i, carry):
        at = pl.ds(pl.multiple_of(i * step, step), step)
        head, tail = vecs[0, at, :], vecs[1, at, :]
        negs = split(vecs[2])
        second = slots[at, :][:, 3:4] > 0.5
        hs = split(head)
        r0, r1 = (rh[0], rl[0]), (rh[1], rl[1])
        projected = jnp.where(second, mm3(hs, r1), mm3(hs, r0))
        ps = split(projected)
        pos_score = jnp.sum(projected * tail, axis=1, keepdims=True)
        neg_score = mm3(ps, negs, last)
        pos_weight = -1.0 / (1.0 + jnp.exp(pos_score))
        neg_weight = (1.0 / (1.0 + jnp.exp(-neg_score))) * (1.0 / edges)
        proj_grad = pos_weight * tail + mm3(split(neg_weight), negs)
        gs = split(proj_grad)
        grads[0, at, :] = jnp.where(second, mm3(gs, r1, last), mm3(gs, r0, last))
        grads[1, at, :] = pos_weight * projected
        grads[2] = grads[2] + mm3(split(neg_weight.T), ps)
        ht = split(head.T)
        g1 = split(jnp.where(second, proj_grad, 0.0))
        g0 = split(jnp.where(second, 0.0, proj_grad))
        whole[0:wide] = whole[0:wide] + mm3(ht, g0)
        whole[wide : 2 * wide] = whole[wide : 2 * wide] + mm3(ht, g1)
        return carry

    lax.fori_loop(0, edges // step, grad, 0)
    rel_grad[0] = whole[0:width, 0:width]
    rel_grad[1] = whole[wide : wide + width, 0:width]

    for s in range(3):
        place = as_row(slots[:, s : s + 1], edges).astype(jnp.int32)
        gh, gl = split(grads[s])

        def spread(i, carry, s=s):
            at = i * 8 * cap
            put = (iota((8 * cap, edges), 0) + at == place).astype(bf16)
            v = mm(put, gh) + mm(put, gl)
            to = pl.ds(i * 8, 8)
            for c in range(full // LANES):
                out[to, c * per + s * cap : c * per + (s + 1) * cap, :] = v[
                    :, c * LANES : (c + 1) * LANES
                ].reshape(8, cap, LANES)
            tails = v[:, full:].reshape(8, 3, 8, LANES)
            packed = jnp.zeros((64, LANES), f32)
            for q in range(3):
                g = 3 * s + q
                part = tails[:, q].reshape(64, LANES)
                if g == 8:
                    out[to, base + 8 : base + 16, :] = part.reshape(8, 8, LANES)
                elif g == 0:
                    packed = packed + part
                else:
                    packed = packed + pltpu.roll(part, 16 * g, 1)
            packed = packed.reshape(8, 8, LANES)
            if s > 0:
                packed = packed + out[to, base : base + 8, :]
            out[to, base : base + 8, :] = packed
            return carry

        lax.fori_loop(0, owners // 8, spread, 0)


def return_kernel(msgs, asked, total, back, acc, xh, xl, send, recv):
    me = lax.axis_index("rows")
    owners = msgs.shape[0]
    nyc = owners // NZ
    rows, width = total.shape
    full = width // LANES * LANES
    slots = 72
    planes = full // LANES
    meet_all(nyc)

    def copy(p, slot):
        return remote(msgs.at[p], back.at[slot], send.at[p], recv.at[slot], p)

    for_others(nyc, 1, lambda p: copy(p, me).start())
    back[me] = msgs[me]
    xh[...] = jnp.zeros(xh.shape, bf16)
    xl[...] = jnp.zeros(xl.shape, bf16)

    def clear(i, carry):
        acc[pl.ds(pl.multiple_of(i * 256, 256), 256), :] = jnp.zeros((256, full + LANES), f32)
        return carry

    lax.fori_loop(0, rows // 256, clear, 0)

    def take(b, carry):
        origin = [partner(b, j, -1, nyc) for j in range(NZ)]
        for j, q in enumerate(origin):
            arrived = copy(q, q)
            if j == 0:
                pl.when(b > 0)(arrived.wait_recv)
            else:
                arrived.wait_recv()
            gap = jnp.zeros((8, LANES), f32)
            for c in range(planes + 1):
                if c < planes:
                    v = back[q, c * slots : (c + 1) * slots, :]
                else:
                    v = unpack_tail(back, q, planes * slots)
                h, l = split(jnp.concatenate([v, gap], axis=0))
                xh[j * LANES : j * LANES + 80, c * LANES : (c + 1) * LANES] = h
                xl[j * LANES : j * LANES + 80, c * LANES : (c + 1) * LANES] = l
        names = [asked[q][0:1, :].astype(jnp.int32) for q in origin]

        def add(m, inner):
            at = pl.ds(pl.multiple_of(m * 256, 256), 256)
            row = iota((256, LANES), 0) + m * 256
            put = jnp.concatenate([(row == name).astype(bf16) for name in names], axis=1)
            acc[at, :] = acc[at, :] + (mm(put, xh[...]) + mm(put, xl[...]))
            return inner

        lax.fori_loop(0, rows // 256, add, 0)
        return carry

    lax.fori_loop(0, nyc, take, 0)

    def store(i, carry):
        at = pl.ds(pl.multiple_of(i * 256, 256), 256)
        total[at, :] = acc[at, :][:, :width]
        return carry

    lax.fori_loop(0, rows // 256, store, 0)
    for_others(nyc, 1, lambda p: copy(p, p).wait_send())


def adagrad_rows(row_block, accum, gradient):
    updated = accum + jnp.mean(gradient * gradient, axis=1)
    return (row_block - entity_rate * gradient / jnp.sqrt(updated)[:, None], updated)


def adagrad_dense(params, accum, gradient):
    updated = accum + gradient * gradient
    return (params - relation_rate * gradient / jnp.sqrt(updated), updated)


def per_device(
    entities,
    entity_state,
    relations,
    relation_state,
    head_block,
    head_row,
    tail_block,
    tail_row,
    rel_slot,
    neg_block,
    neg_row,
):
    owners = lax.axis_size("rows")
    edges = head_row.shape[0]
    rows, width = entities.shape
    full = width // LANES * LANES
    wide = full + LANES
    cap = 3 * edges // owners
    message = full // LANES * 3 * cap + 16
    vmem = pl.BlockSpec(memory_space=pltpu.VMEM)
    shape = jax.ShapeDtypeStruct
    params = functools.partial(pltpu.CompilerParams, vmem_limit_bytes=VMEM_LIMIT)
    dma = pltpu.SemaphoreType.DMA((owners,))

    rows_in = jnp.stack([head_row, tail_row, neg_row, rel_slot])
    want, slots = pl.pallas_call(
        functools.partial(route_kernel, cap),
        out_shape=(shape((owners, 8, LANES), f32), shape((edges, LANES), f32)),
        in_specs=[vmem] * 4,
        out_specs=(vmem, vmem),
        compiler_params=params(),
        name="route",
    )(head_block, tail_block, neg_block, rows_in)

    fetched, asked = pl.pallas_call(
        fetch_kernel,
        out_shape=(shape((owners, message, LANES), f32), shape((owners, 8, LANES), f32)),
        in_specs=[vmem] * 2,
        out_specs=(vmem, vmem),
        scratch_shapes=[
            pltpu.VMEM((rows, wide), bf16),
            pltpu.VMEM((rows, wide), bf16),
            pltpu.VMEM((owners, message, LANES), f32),
            dma,
            dma,
            dma,
            dma,
        ],
        compiler_params=params(collective_id=0, has_side_effects=True),
        name="fetch",
    )(want, entities)

    out, rel_grad = pl.pallas_call(
        edge_kernel,
        out_shape=(shape((owners, message, LANES), f32), shape(relations.shape, f32)),
        in_specs=[vmem] * 3,
        out_specs=(vmem, vmem),
        scratch_shapes=[
            pltpu.VMEM((owners * cap, wide), bf16),
            pltpu.VMEM((owners * cap, wide), bf16),
            pltpu.VMEM((3, edges, wide), f32),
            pltpu.VMEM((3, edges, wide), f32),
            pltpu.VMEM((2 * wide, wide), f32),
            pltpu.VMEM((2, wide, wide), bf16),
            pltpu.VMEM((2, wide, wide), bf16),
        ],
        compiler_params=params(),
        name="edges",
    )(fetched, relations, slots)

    partial_grad = pl.pallas_call(
        return_kernel,
        out_shape=shape(entities.shape, f32),
        in_specs=[vmem] * 2,
        out_specs=vmem,
        scratch_shapes=[
            pltpu.VMEM((owners, message, LANES), f32),
            pltpu.VMEM((rows, wide), f32),
            pltpu.VMEM((NZ * LANES, wide), bf16),
            pltpu.VMEM((NZ * LANES, wide), bf16),
            dma,
            dma,
        ],
        compiler_params=params(collective_id=1, has_side_effects=True),
        name="give_back",
    )(out, asked)

    rel_summed = lax.psum(rel_grad, "rows")
    summed = lax.psum(partial_grad, "rel")
    new_entities, new_entity_state = adagrad_rows(entities, entity_state, summed)
    new_relations, new_relation_state = adagrad_dense(relations, relation_state, rel_summed)
    return (new_entities, new_entity_state, new_relations, new_relation_state)


def solution(mesh):
    placed = (
        P("rows", None),
        P("rows"),
        P("rel", None, None),
        P("rel", None, None),
        P(("rows", "rel"), None),
        P(("rows", "rel")),
        P(("rows", "rel"), None),
        P(("rows", "rel")),
        P(("rows", "rel")),
        P(("rows", "rel"), None),
        P(("rows", "rel")),
    )
    return jax.shard_map(
        per_device,
        mesh=mesh,
        in_specs=placed,
        out_specs=(P("rows", None), P("rows"), P("rel", None, None), P("rel", None, None)),
        check_vma=False,
    )
```

```python
import functools

import jax
import jax.numpy as jnp
from jax import lax
from jax.experimental import pallas as pl
from jax.experimental.pallas import tpu as pltpu
from jax.sharding import PartitionSpec as P

MESH = pl.DeviceIdType.MESH
entity_rate = 0.1
relation_rate = 0.1
LANES = 128
NZ = 8
VMEM_LIMIT = 56 * 2**20
f32, bf16 = jnp.float32, jnp.bfloat16


def split(x):
    hi = x.astype(bf16)
    return hi, (x - hi.astype(f32)).astype(bf16)


def mm(a, b, dims=((1,), (0,))):
    return lax.dot_general(a, b, (dims, ((), ())), preferred_element_type=f32)


def mm3(a, b, dims=((1,), (0,))):
    ah, al = a
    bh, bl = b
    return mm(ah, bh, dims) + (mm(ah, bl, dims) + mm(al, bh, dims))


def iota(shape, axis):
    return lax.broadcasted_iota(jnp.int32, shape, axis)


def as_column(row, n):
    return jnp.sum(
        jnp.where(iota((n, n), 0) == iota((n, n), 1), jnp.broadcast_to(row, (n, n)), 0.0),
        axis=1,
        keepdims=True,
    )


def as_row(column, n):
    return jnp.sum(
        jnp.where(iota((n, n), 0) == iota((n, n), 1), jnp.broadcast_to(column, (n, n)), 0.0),
        axis=0,
        keepdims=True,
    )


def route_kernel(cap, hb, tb, nb, hr, tr, nr, rel_slot, want_ref, slot_ref):
    n = hb.shape[1]
    owners = want_ref.shape[0]
    before = (iota((n, n), 1) < iota((n, n), 0)).astype(bf16)
    lists = jnp.zeros((owners, LANES), f32)
    slots = jnp.zeros((n, LANES), f32)
    lane = iota((n, LANES), 1).astype(f32)
    for s, (ref, row) in enumerate(((hb, hr), (tb, tr), (nb, nr))):
        block_row = ref[...].astype(f32)
        block = as_column(block_row, n)
        member = lane == block
        earlier = mm(before, member.astype(bf16))
        pos = jnp.sum(jnp.where(member, earlier, 0.0), axis=1, keepdims=True)
        slots = jnp.where(lane == s, block * cap + pos, slots)
        value = as_column(row[...].astype(f32), n) + 1.0
        high = jnp.floor(value * (1.0 / 64.0))
        low = value - 64.0 * high
        at = lane == pos + float(cap * s)
        to_owner = (iota((owners, n), 0).astype(f32) == block_row).astype(bf16)
        lists = (
            lists
            + 64.0 * mm(to_owner, jnp.where(at, high, 0.0).astype(bf16))
            + mm(to_owner, jnp.where(at, low, 0.0).astype(bf16))
        )
    slots = jnp.where(lane == 3, as_column(rel_slot[...].astype(f32), n), slots)
    want_ref[...] = jnp.broadcast_to((lists - 1.0)[:, None, :], want_ref.shape)
    slot_ref[...] = slots


def partner(b, j, sign, nyc):
    me = lax.axis_index("rows")
    z, yc = me // nyc, me % nyc
    dz = (j + 1) // 2 if j % 2 else (NZ - j // 2) % NZ
    if sign > 0:
        return ((z + dz) % NZ) * nyc + (yc + b + j) % nyc
    return ((z + NZ - dz) % NZ) * nyc + (yc + 2 * nyc - b - j % nyc) % nyc


def meet_all(nyc, beside=()):
    barrier = pltpu.get_barrier_semaphore()
    for p in beside:
        pl.semaphore_signal(barrier, inc=1, device_id={"rel": p}, device_id_type=MESH)

    def greet(b, carry):
        for j in range(NZ):
            p = partner(b, j, 1, nyc)

            def tell():
                pl.semaphore_signal(barrier, inc=1, device_id={"rows": p}, device_id_type=MESH)

            if j == 0:
                pl.when(b > 0)(tell)
            else:
                tell()
        return carry

    lax.fori_loop(0, nyc, greet, 0)
    pl.semaphore_wait(barrier, NZ * nyc - 1 + len(beside))


def for_others(nyc, sign, body):
    def step(b, carry):
        for j in range(NZ):
            p = partner(b, j, sign, nyc)
            if j == 0:
                pl.when(b > 0)(functools.partial(body, p))
            else:
                body(p)
        return carry

    lax.fori_loop(0, nyc, step, 0)


def remote(src, dst, send, recv, p):
    return pltpu.make_async_remote_copy(
        src_ref=src, dst_ref=dst, send_sem=send, recv_sem=recv, device_id={"rows": p}, device_id_type=MESH
    )


def fetch_kernel(
    want, ent, fetched, asked, hi, lo, stage, isend, irecv, send, recv
):
    me = lax.axis_index("rows")
    owners = want.shape[0]
    nyc = owners // NZ
    width, rows = ent.shape
    full = width // LANES * LANES
    slots = 72
    meet_all(nyc)

    def index_copy(p, slot):
        return remote(want.at[p], asked.at[slot], isend.at[p], irecv.at[slot], p)

    for_others(nyc, 1, lambda p: index_copy(p, me).start())
    asked[me] = want[me]

    def cut(i, carry):
        at = pl.ds(pl.multiple_of(i * 256, 256), 256)
        for c in range(full // LANES + 1):
            h, l = split(plane_of(ent, c, at))
            hi[at, c * LANES : (c + 1) * LANES] = h
            lo[at, c * LANES : (c + 1) * LANES] = l
        return carry

    lax.fori_loop(0, rows // 256, cut, 0)
    for_others(nyc, 1, lambda p: index_copy(p, p).wait_recv())
    chunk = 512

    def answer(b, carry):
        to = [partner(b, j, 1, nyc) for j in range(NZ)]
        ids = jnp.concatenate([as_column(asked[p][0:1, :], LANES)[:slots] for p in to], axis=0)
        ids = ids.astype(jnp.int32)

        def gather(c, total):
            at = pl.ds(pl.multiple_of(c * chunk, chunk), chunk)
            pick = (ids - c * chunk == iota((NZ * slots, chunk), 1)).astype(bf16)
            return total + (mm(pick, hi[at, :]) + mm(pick, lo[at, :]))

        found = lax.fori_loop(
            0, rows // chunk, gather, jnp.zeros((NZ * slots, full + LANES), f32)
        )
        for j, p in enumerate(to):
            pack(stage, p, found[j * slots : (j + 1) * slots])
            copy = remote(stage.at[p], fetched.at[me], send.at[p], recv.at[me], p)
            if j == 0:
                pl.when(b > 0)(copy.start)
            else:
                copy.start()
        return carry

    lax.fori_loop(0, nyc, answer, 0)
    fetched[me] = stage[me]

    def finish(p):
        index_copy(p, p).wait_send()
        copy = remote(stage.at[p], fetched.at[p], send.at[p], recv.at[p], p)
        copy.wait_send()
        copy.wait_recv()

    for_others(nyc, 1, finish)


def plane_of(turned, c, at):
    part = turned[c * LANES : min((c + 1) * LANES, turned.shape[0]), at]
    if part.shape[0] < LANES:
        gap = jnp.zeros((LANES - part.shape[0], part.shape[1]), part.dtype)
        part = jnp.concatenate([part, gap], axis=0)
    return part.T


def pack_tail(tail):
    packed = tail[0:8]
    for g in range(1, 8):
        packed = packed + pltpu.roll(tail[8 * g : 8 * g + 8], 16 * g, 1)
    return packed


def open_tail(packed):
    low = iota((8, LANES), 1) < 16
    parts = [jnp.where(low, packed, 0.0)]
    for g in range(1, 8):
        parts.append(jnp.where(low, pltpu.roll(packed, LANES - 16 * g, 1), 0.0))
    return jnp.concatenate(parts, axis=0)


def pack(ref, p, block):
    slots = block.shape[0]
    planes = block.shape[1] // LANES - 1
    for c in range(planes):
        ref[p, c * slots : (c + 1) * slots, :] = block[:, c * LANES : (c + 1) * LANES]
    tail = block[:, planes * LANES :]
    ref[p, planes * slots : planes * slots + 8, :] = pack_tail(tail)
    ref[p, planes * slots + 8 : planes * slots + 16, :] = tail[64:72]


def unpack_tail(ref, p, base):
    return jnp.concatenate(
        [open_tail(ref[p, base : base + 8, :]), ref[p, base + 8 : base + 16, :]], axis=0
    )


def edge_kernel(
    fetched, rel, slots, out, rel_grad, xh, xl, vecs, grads, whole, rh, rl
):
    owners = fetched.shape[0]
    edges = slots.shape[0]
    width = rel.shape[1]
    full = width // LANES * LANES
    wide = full + LANES
    cap = 3 * edges // owners
    per = 3 * cap
    base = full // LANES * per
    total = owners * cap
    step = min(256, edges)
    low8 = iota((8, LANES), 1) < 16

    rh[...] = jnp.zeros(rh.shape, bf16)
    rl[...] = jnp.zeros(rl.shape, bf16)
    for k in range(rel.shape[0]):
        h, l = split(rel[k])
        rh[k, :width, :width] = h
        rl[k, :width, :width] = l

    for s in range(3):

        def collect(i, carry, s=s):
            at = pl.ds(pl.multiple_of(i * 8 * cap, 8 * cap), 8 * cap)
            from_ = pl.ds(i * 8, 8)
            for c in range(full // LANES):
                v = fetched[from_, c * per + s * cap : c * per + (s + 1) * cap, :]
                h, l = split(v.reshape(8 * cap, LANES))
                xh[at, c * LANES : (c + 1) * LANES] = h
                xl[at, c * LANES : (c + 1) * LANES] = l
            packed = fetched[from_, base : base + 8, :].reshape(64, LANES)
            low = iota((64, LANES), 1) < 16
            parts = []
            for g in range(3 * s, 3 * s + 3):
                if g == 8:
                    part = fetched[from_, base + 8 : base + 16, :].reshape(64, LANES)
                elif g == 0:
                    part = jnp.where(low, packed, 0.0)
                else:
                    part = jnp.where(low, pltpu.roll(packed, LANES - 16 * g, 1), 0.0)
                parts.append(part.reshape(8, 1, 8, LANES))
            h, l = split(jnp.concatenate(parts, axis=1).reshape(8 * cap, LANES))
            xh[at, full:] = h
            xl[at, full:] = l
            return carry

        lax.fori_loop(0, owners // 8, collect, 0)

        def choose(i, carry, s=s):
            at = pl.ds(pl.multiple_of(i * step, step), step)
            place = slots[at, :][:, s : s + 1].astype(jnp.int32)
            pick = (place == iota((step, total), 1)).astype(bf16)
            vecs[s, at, :] = mm(pick, xh[...]) + mm(pick, xl[...])
            return carry

        lax.fori_loop(0, edges // step, choose, 0)

    grads[2] = jnp.zeros((edges, wide), f32)
    whole[0:wide] = jnp.zeros((wide, wide), f32)
    whole[wide : 2 * wide] = jnp.zeros((wide, wide), f32)
    last = ((1,), (1,))

    def grad(i, carry):
        at = pl.ds(pl.multiple_of(i * step, step), step)
        head, tail = vecs[0, at, :], vecs[1, at, :]
        negs = split(vecs[2])
        second = slots[at, :][:, 3:4] > 0.5
        hs = split(head)
        r0, r1 = (rh[0], rl[0]), (rh[1], rl[1])
        projected = jnp.where(second, mm3(hs, r1), mm3(hs, r0))
        ps = split(projected)
        pos_score = jnp.sum(projected * tail, axis=1, keepdims=True)
        neg_score = mm3(ps, negs, last)
        pos_weight = -1.0 / (1.0 + jnp.exp(pos_score))
        neg_weight = (1.0 / (1.0 + jnp.exp(-neg_score))) * (1.0 / edges)
        proj_grad = pos_weight * tail + mm3(split(neg_weight), negs)
        gs = split(proj_grad)
        grads[0, at, :] = jnp.where(second, mm3(gs, r1, last), mm3(gs, r0, last))
        grads[1, at, :] = pos_weight * projected
        grads[2] = grads[2] + mm3(split(neg_weight.T), ps)
        ht = split(head.T)
        g1 = split(jnp.where(second, proj_grad, 0.0))
        g0 = split(jnp.where(second, 0.0, proj_grad))
        whole[0:wide] = whole[0:wide] + mm3(ht, g0)
        whole[wide : 2 * wide] = whole[wide : 2 * wide] + mm3(ht, g1)
        return carry

    lax.fori_loop(0, edges // step, grad, 0)
    rel_grad[0] = whole[0:width, 0:width]
    rel_grad[1] = whole[wide : wide + width, 0:width]

    for s in range(3):
        place = as_row(slots[:, s : s + 1], edges).astype(jnp.int32)
        gh, gl = split(grads[s])

        def spread(i, carry, s=s):
            at = i * 8 * cap
            put = (iota((8 * cap, edges), 0) + at == place).astype(bf16)
            v = mm(put, gh) + mm(put, gl)
            to = pl.ds(i * 8, 8)
            for c in range(full // LANES):
                out[to, c * per + s * cap : c * per + (s + 1) * cap, :] = v[
                    :, c * LANES : (c + 1) * LANES
                ].reshape(8, cap, LANES)
            tails = v[:, full:].reshape(8, 3, 8, LANES)
            packed = jnp.zeros((64, LANES), f32)
            for q in range(3):
                g = 3 * s + q
                part = tails[:, q].reshape(64, LANES)
                if g == 8:
                    out[to, base + 8 : base + 16, :] = part.reshape(8, 8, LANES)
                elif g == 0:
                    packed = packed + part
                else:
                    packed = packed + pltpu.roll(part, 16 * g, 1)
            packed = packed.reshape(8, 8, LANES)
            if s > 0:
                packed = packed + out[to, base : base + 8, :]
            out[to, base : base + 8, :] = packed
            return carry

        lax.fori_loop(0, owners // 8, spread, 0)


def return_kernel(
    msgs, asked, ent, state, out, new_state, back, acc, xh, xl, part, land, done, send, recv, xsend, xrecv
):
    me = lax.axis_index("rows")
    owners = msgs.shape[0]
    nyc = owners // NZ
    width, rows = ent.shape
    full = width // LANES * LANES
    slots = 72
    planes = full // LANES
    here = lax.axis_index("rel")
    right, left, across = (here + 1) % 4, (here + 3) % 4, (here + 2) % 4
    meet_all(nyc, (right, left))

    def copy(p, slot):
        return remote(msgs.at[p], back.at[slot], send.at[p], recv.at[slot], p)

    for_others(nyc, 1, lambda p: copy(p, me).start())
    back[me] = msgs[me]
    xh[...] = jnp.zeros(xh.shape, bf16)
    xl[...] = jnp.zeros(xl.shape, bf16)

    def clear(i, carry):
        acc[pl.ds(pl.multiple_of(i * 256, 256), 256), :] = jnp.zeros((256, full + LANES), f32)
        return carry

    lax.fori_loop(0, rows // 256, clear, 0)

    def take(b, carry):
        origin = [partner(b, j, -1, nyc) for j in range(NZ)]
        for j, q in enumerate(origin):
            arrived = copy(q, q)
            if j == 0:
                pl.when(b > 0)(arrived.wait_recv)
            else:
                arrived.wait_recv()
            gap = jnp.zeros((8, LANES), f32)
            for c in range(planes + 1):
                if c < planes:
                    v = back[q, c * slots : (c + 1) * slots, :]
                else:
                    v = unpack_tail(back, q, planes * slots)
                h, l = split(jnp.concatenate([v, gap], axis=0))
                xh[j * LANES : j * LANES + 80, c * LANES : (c + 1) * LANES] = h
                xl[j * LANES : j * LANES + 80, c * LANES : (c + 1) * LANES] = l
        names = [asked[q][0:1, :].astype(jnp.int32) for q in origin]

        def add(m, inner):
            at = pl.ds(pl.multiple_of(m * 256, 256), 256)
            row = iota((256, LANES), 0) + m * 256
            put = jnp.concatenate([(row == name).astype(bf16) for name in names], axis=1)
            acc[at, :] = acc[at, :] + (mm(put, xh[...]) + mm(put, xl[...]))
            return inner

        lax.fori_loop(0, rows // 256, add, 0)
        return carry

    lax.fori_loop(0, nyc, take, 0)

    half = rows // 8
    tails = planes * half
    states = tails + half // 8

    def lay(i, carry):
        at = pl.ds(pl.multiple_of(i * half, half), half)
        for c in range(planes):
            part[i, c * half : (c + 1) * half, :] = acc[at, c * LANES : (c + 1) * LANES]
        tail = acc[at, full:]
        for u in range(half // 64):
            part[i, tails + 8 * u : tails + 8 * u + 8, :] = pack_tail(tail[64 * u : 64 * u + 64])
        part[i, states : states + 8, :] = jnp.zeros((8, LANES), f32)
        return carry

    lax.fori_loop(0, 8, lay, 0)

    def xcopy(k, src, dst, to):
        return pltpu.make_async_remote_copy(
            src_ref=src,
            dst_ref=dst,
            send_sem=xsend.at[k],
            recv_sem=xrecv.at[k],
            device_id={"rel": to},
            device_id_type=MESH,
        )

    sums = [
        xcopy(0, part.at[2 * across], land.at[0], left),
        xcopy(1, part.at[2 * across + 1], land.at[1], right),
        xcopy(2, part.at[2 * left + 1], land.at[2], left),
        xcopy(3, part.at[2 * right], land.at[3], right),
        xcopy(4, part.at[2 * left], land.at[4], left),
        xcopy(5, part.at[2 * right + 1], land.at[5], right),
    ]
    for k in range(4):
        sums[k].start()
    sums[0].wait_recv()
    part[2 * left] = part[2 * left] + land[0]
    sums[4].start()
    sums[1].wait_recv()
    part[2 * right + 1] = part[2 * right + 1] + land[1]
    sums[5].start()

    def update(h, first, second):
        i = 2 * here + h
        done[i, states : states + 8, :] = jnp.zeros((8, LANES), f32)
        for u in range(half // LANES):

            def summed(a, n):
                return part[i, a : a + n, :] + land[first, a : a + n, :] + land[second, a : a + n, :]

            at = pl.ds(pl.multiple_of(i * half + u * LANES, LANES), LANES)
            grad = [summed(c * half + u * LANES, LANES) for c in range(planes)]
            packed = summed(tails + 16 * u, 16)
            grad.append(jnp.concatenate([open_tail(packed[0:8]), open_tail(packed[8:16])], axis=0))
            squares = sum(g * g for g in grad)
            before = as_column(state[pl.ds(i * (half // LANES) + u, 1), :], LANES)
            after = before + jnp.sum(squares, axis=1, keepdims=True) * (1.0 / width)
            rate = entity_rate / jnp.sqrt(after)
            for c, g in enumerate(grad):
                new = plane_of(ent, c, at) - rate * g
                if c < planes:
                    done[i, c * half + u * LANES : c * half + (u + 1) * LANES, :] = new
                else:
                    for w in range(2):
                        k = tails + 16 * u + 8 * w
                        done[i, k : k + 8, :] = pack_tail(new[64 * w : 64 * w + 64])
            done[i, states + u : states + u + 1, :] = as_row(after, LANES)
        return i

    def spread(k, i, to):
        return xcopy(k, done.at[i], done.at[i], to)

    def write(i):
        at = pl.ds(pl.multiple_of(i * half, half), half)
        for c in range(planes):
            out[c * LANES : (c + 1) * LANES, at] = done[i, c * half : (c + 1) * half, :].T
        tail = jnp.concatenate(
            [open_tail(done[i, tails + 8 * u : tails + 8 * u + 8, :]) for u in range(half // 64)], axis=0
        )
        out[full:width, at] = tail.T[0 : width - full]
        new_state[i] = done[i, states : states + 8, :]

    sums[3].wait_recv()
    sums[4].wait_recv()
    mine = update(0, 3, 4)
    spread(6, mine, left).start()
    spread(7, mine, right).start()
    sums[2].wait_recv()
    sums[5].wait_recv()
    mine = update(1, 2, 5)
    spread(8, mine, left).start()
    spread(9, mine, right).start()
    write(2 * here)
    write(2 * here + 1)
    spread(7, 2 * left, right).wait_recv()
    spread(10, 2 * left, right).start()
    write(2 * left)
    spread(8, 2 * right + 1, left).wait_recv()
    spread(11, 2 * right + 1, left).start()
    write(2 * right + 1)
    spread(6, 2 * right, left).wait_recv()
    write(2 * right)
    spread(9, 2 * left + 1, right).wait_recv()
    write(2 * left + 1)
    spread(10, 2 * across, right).wait_recv()
    write(2 * across)
    spread(11, 2 * across + 1, left).wait_recv()
    write(2 * across + 1)
    for k in range(6):
        sums[k].wait_send()
    for k, i in ((6, 2 * here), (7, 2 * here), (8, 2 * here + 1), (9, 2 * here + 1)):
        spread(k, i, left).wait_send()
    spread(10, 2 * left, right).wait_send()
    spread(11, 2 * right + 1, left).wait_send()
    for_others(nyc, 1, lambda p: copy(p, p).wait_send())


def adagrad_dense(params, accum, gradient):
    updated = accum + gradient * gradient
    return (params - relation_rate * gradient / jnp.sqrt(updated), updated)


def per_device(
    entities,
    entity_state,
    relations,
    relation_state,
    head_block,
    head_row,
    tail_block,
    tail_row,
    rel_slot,
    neg_block,
    neg_row,
):
    owners = lax.axis_size("rows")
    edges = head_row.shape[0]
    rows, width = entities.shape
    full = width // LANES * LANES
    wide = full + LANES
    cap = 3 * edges // owners
    message = full // LANES * 3 * cap + 16
    vmem = pl.BlockSpec(memory_space=pltpu.VMEM)
    shape = jax.ShapeDtypeStruct
    params = functools.partial(pltpu.CompilerParams, vmem_limit_bytes=VMEM_LIMIT)
    dma = pltpu.SemaphoreType.DMA((owners,))

    lanes = [
        a.reshape(1, edges)
        for a in (head_block, tail_block, neg_block, head_row, tail_row, neg_row, rel_slot)
    ]
    want, slots = pl.pallas_call(
        functools.partial(route_kernel, cap),
        out_shape=(shape((owners, 8, LANES), f32), shape((edges, LANES), f32)),
        in_specs=[vmem] * 7,
        out_specs=(vmem, vmem),
        compiler_params=params(),
        name="route",
    )(*lanes)

    fetched, asked = pl.pallas_call(
        fetch_kernel,
        out_shape=(shape((owners, message, LANES), f32), shape((owners, 8, LANES), f32)),
        in_specs=[vmem] * 2,
        out_specs=(vmem, vmem),
        scratch_shapes=[
            pltpu.VMEM((rows, wide), bf16),
            pltpu.VMEM((rows, wide), bf16),
            pltpu.VMEM((owners, message, LANES), f32),
            dma,
            dma,
            dma,
            dma,
        ],
        compiler_params=params(collective_id=0, has_side_effects=True),
        name="fetch",
    )(want, entities.T)

    out, rel_grad = pl.pallas_call(
        edge_kernel,
        out_shape=(shape((owners, message, LANES), f32), shape(relations.shape, f32)),
        in_specs=[vmem] * 3,
        out_specs=(vmem, vmem),
        scratch_shapes=[
            pltpu.VMEM((owners * cap, wide), bf16),
            pltpu.VMEM((owners * cap, wide), bf16),
            pltpu.VMEM((3, edges, wide), f32),
            pltpu.VMEM((3, edges, wide), f32),
            pltpu.VMEM((2 * wide, wide), f32),
            pltpu.VMEM((2, wide, wide), bf16),
            pltpu.VMEM((2, wide, wide), bf16),
        ],
        compiler_params=params(),
        name="edges",
    )(fetched, relations, slots)

    rel_summed = lax.psum(rel_grad, "rows")
    block = full // LANES * (rows // 8) + rows // 64 + 8
    turned, states = pl.pallas_call(
        return_kernel,
        out_shape=(shape((width, rows), f32), shape((8, 8, LANES), f32)),
        in_specs=[vmem] * 4,
        out_specs=(vmem, vmem),
        scratch_shapes=[
            pltpu.VMEM((owners, message, LANES), f32),
            pltpu.VMEM((rows, wide), f32),
            pltpu.VMEM((NZ * LANES, wide), bf16),
            pltpu.VMEM((NZ * LANES, wide), bf16),
            pltpu.VMEM((8, block, LANES), f32),
            pltpu.VMEM((6, block, LANES), f32),
            pltpu.VMEM((8, block, LANES), f32),
            dma,
            dma,
            pltpu.SemaphoreType.DMA((12,)),
            pltpu.SemaphoreType.DMA((12,)),
        ],
        compiler_params=params(collective_id=1, has_side_effects=True),
        name="give_back",
    )(out, asked, entities.T, entity_state.reshape(rows // LANES, LANES))

    new_entities = turned.T
    new_entity_state = states[:, : rows // 8 // LANES].reshape(rows)
    new_relations, new_relation_state = adagrad_dense(relations, relation_state, rel_summed)
    return (new_entities, new_entity_state, new_relations, new_relation_state)


def solution(mesh):
    placed = (
        P("rows", None),
        P("rows"),
        P("rel", None, None),
        P("rel", None, None),
        P(("rows", "rel"), None),
        P(("rows", "rel")),
        P(("rows", "rel"), None),
        P(("rows", "rel")),
        P(("rows", "rel")),
        P(("rows", "rel"), None),
        P(("rows", "rel")),
    )
    return jax.shard_map(
        per_device,
        mesh=mesh,
        in_specs=placed,
        out_specs=(P("rows", None), P("rows"), P("rel", None, None), P("rel", None, None)),
        check_vma=False,
    )
```
